32 devices in a mesh: stn: 16 (over z, y, core), tm: 2 (over x).
Axes of the slice: x: 2, y: 2, z: 4, core: 2. Of those that a mesh axis runs over, the one named last changes fastest.
Arguments:
- voltages: bfloat16 [2, 1024, 131072], P(None, 'stn', 'tm'), may hold values from -6 to 6
- filter_taps: float32 [16, 4096], replicated, may hold values from -1.5 to 1.5
- membership: int32 [32, 512], P('stn'), may hold values from 0 to 3
- block_active: int32 [32, 10], P('stn'), may hold values 0 or 1
Outputs:
- visibilities: float32 [32, 10, 2, 256, 256], P('stn', None, None, 'tm')
The draws below stay inside these ranges and needn't reach their ends.
All inputs are finite; a program needn't handle non-finite values. No bound on the sum of `block_active` on one device may be relied on, other than what follows from the above.
Results may differ from the reference program's by a relative error of at most 0.006.
Values may be sent and summed in bfloat16 or wider, within the bound.
A program may use at most 256 MiB of HBM per device.

```python
import math
import jax
import jax.numpy as jnp
import numpy as np
from jax import lax

STATIONS = 512
INPUTS = 1024
TAPS = 16
RADIX = 64
FFT = 4096
AVG = 16
CHANNELS = 32
FINE = 512
F_DEV = 16
FRAMES = 32
SAMPLES = 131072
BLOCK = 256
PAIRS = 10
N_TM = 2


def place_ends(entries, own_key, low, top_value):
    longest = entries.shape.index(max(entries.shape))
    spots = []
    for shift in (0, 1):
        where = [jax.random.randint(jax.random.fold_in(own_key, axis), (), 0, length) for axis, length in enumerate(entries.shape)]
        where[longest] = (where[longest] + shift) % entries.shape[longest]
        spots.append(tuple(where))
    return entries.at[spots[0]].set(low).at[spots[1]].set(top_value)


def shard_levels(rng, shape, cuts, smallest, high):
    level = 1.0
    for dim, parts in cuts:
        heights = jax.random.uniform(jax.random.fold_in(jax.random.fold_in(rng, 6), dim), (parts,), jnp.float32, smallest / len(cuts), high / len(cuts))
        level = level * jnp.repeat(jnp.exp(heights), shape[dim] // parts).reshape((-1,) + (1,) * (len(shape) - 1 - dim))
    return level


def bell_draw(own_key, shape, deviation, reach, shards=(), held_as=jnp.bfloat16):
    values = deviation * jax.random.normal(own_key, shape, jnp.float32)
    if shards:
        values = values * shard_levels(own_key, shape, shards, -0.22, 0.18)
    return jnp.clip(values, -reach, reach).astype(held_as)


def setup_inputs(seed: int = 0) -> dict:
    splits = jax.random.split(jax.random.key(seed), 5)
    voltages = bell_draw(splits[0], (2, INPUTS, SAMPLES), 1.0, 6.0, ((1, 16), (2, 2)))
    filter_taps = bell_draw(splits[1], (TAPS, FFT), TAPS ** -0.5, 1.5, (), jnp.float32)
    membership = place_ends(jax.random.randint(splits[2], (CHANNELS, STATIONS), 0, 4), jax.random.fold_in(splits[2], 1), 0, 3).astype(jnp.int32)
    block_active = place_ends((jax.random.randint(splits[3], (CHANNELS, PAIRS), 0, 2) < 1).astype(jnp.int32), jax.random.fold_in(splits[3], 1), 0, 1)
    return {"voltages": voltages, "filter_taps": filter_taps, "membership": membership, "block_active": block_active}


def pair_tables(count):
    upper_list = []
    lower_list = []
    for upper in range(count):
        for lower in range(upper + 1):
            upper_list.append(upper)
            lower_list.append(lower)
    return np.array(upper_list, dtype=np.int32), np.array(lower_list, dtype=np.int32)


def reference(voltages, filter_taps, membership, block_active):
    group_width = math.gcd(INPUTS, 32)
    group_count = INPUTS // group_width
    bins = ((np.arange(FINE) - RADIX * (FINE // (2 * RADIX))) % FFT).astype(np.int32)

    def channelize(group_index):
        group = lax.dynamic_slice_in_dim(voltages, group_index * group_width, group_width, 1)
        frames = group.astype(jnp.float32).reshape(2, group_width, FRAMES, FFT)
        padded = jnp.concatenate([jnp.zeros((2, group_width, TAPS - 1, FFT), jnp.float32), frames], axis=2)
        filtered = jnp.zeros((2, group_width, FRAMES, FFT), jnp.float32)
        for tap_index in range(TAPS):
            filtered = filtered + filter_taps[tap_index] * padded[:, :, tap_index:tap_index + FRAMES, :]
        signal = lax.complex(filtered[0], filtered[1])
        transformed = jnp.fft.fft(signal, axis=-1) / RADIX
        picked = transformed[:, :, bins]
        stacked = jnp.stack([jnp.real(picked), jnp.imag(picked)], axis=1)
        return stacked.astype(jnp.bfloat16)

    spectra = lax.map(channelize, jnp.arange(group_count, dtype=jnp.int32))
    spectra = spectra.reshape(INPUTS, 2, FRAMES, FINE)

    upper_tab, lower_tab = pair_tables(INPUTS // BLOCK)
    block_count = INPUTS // BLOCK
    scale = 1.0 / (AVG * FRAMES)

    def correlate(channel):
        piece = lax.dynamic_slice_in_dim(spectra, channel * AVG, AVG, 3)
        station_ids = lax.dynamic_index_in_dim(membership, channel, 0, keepdims=False)
        per_input = jnp.repeat(station_ids, 2)
        same = (per_input[:, None] == per_input[None, :]).astype(jnp.float32)
        active = lax.dynamic_index_in_dim(block_active, channel, 0, keepdims=False).astype(jnp.float32)
        mask = same.reshape(block_count, BLOCK, block_count, BLOCK)[upper_tab, :, lower_tab, :]
        mask = mask * active[:, None, None]
        total = jnp.zeros((PAIRS, 2, BLOCK, BLOCK), jnp.float32)
        for block_time in range(N_TM):
            part = piece[:, :, block_time * F_DEV:(block_time + 1) * F_DEV, :].astype(jnp.float32)
            real_in = part[:, 0].reshape(INPUTS, F_DEV * AVG)
            imag_in = part[:, 1].reshape(INPUTS, F_DEV * AVG)
            left = jnp.concatenate([real_in, imag_in], axis=1)
            swapped = jnp.concatenate([imag_in, -real_in], axis=1)
            real_prod = jnp.dot(left, left.T, precision=lax.Precision.HIGHEST)
            imag_prod = jnp.dot(swapped, left.T, precision=lax.Precision.HIGHEST)
            gram = jnp.stack([real_prod, imag_prod]) * scale
            picked = gram.reshape(2, block_count, BLOCK, block_count, BLOCK)[:, upper_tab, :, lower_tab, :]
            partial_value = (picked * mask[:, None]).astype(jnp.bfloat16)
            partial_value = lax.optimization_barrier(partial_value)
            total = total + partial_value.astype(jnp.float32)
        return total

    return lax.map(correlate, jnp.arange(CHANNELS, dtype=jnp.int32))
```

```python
import math

import jax
import jax.numpy as jnp
import numpy as np
from jax import lax
from jax.experimental import pallas as pl
from jax.experimental.pallas import tpu as pltpu
from jax.sharding import PartitionSpec as P

RADIX = 64
AVG = 16
BLOCKS = 4
ROWS = 16
LANES = 128
SPLIT = 4


def dft_table(fft, bins):
    quarter = fft // SPLIT
    count = bins // SPLIT
    n = np.arange(quarter)[:, None]
    parts = []
    for r in range(SPLIT):
        k = SPLIT * np.arange(count)[None, :] + r - bins // 2
        angle = 2.0 * math.pi * ((n * k) % fft) / fft
        c, s = np.cos(angle) / RADIX, np.sin(angle) / RADIX
        parts.append(np.block([[c, -s], [s, c]]))
    return np.stack(parts).astype(np.float32).astype(jnp.bfloat16)


def fir_dft_kernel(taps, frames, fft, v_ref, h_ref, w_ref, own_ref, halo_ref, filt, y_ref):
    quarter = fft // SPLIT
    outs = frames + taps - 1

    def chunk(g, carry):
        base = pl.multiple_of(g * LANES, LANES)
        for c in range(2):
            for q in range(SPLIT):
                at = [
                    pl.multiple_of(j * fft + q * quarter + base, LANES) for j in range(frames)
                ]
                v = [
                    v_ref[c, :, pl.ds(a, LANES)].astype(jnp.float32).reshape(2, 8, LANES)
                    for a in at
                ]
                col = pl.multiple_of(q * quarter + base, LANES)
                h = [h_ref[t, :, pl.ds(col, LANES)][None] for t in range(taps)]
                for m in range(outs):
                    acc = None
                    for j in range(max(0, m - taps + 1), min(frames - 1, m) + 1):
                        term = h[j - m + taps - 1] * v[j]
                        acc = term if acc is None else acc + term
                    filt[c, q, m] = acc.reshape(ROWS, LANES)
        for m in range(outs):
            z = [[filt[c, q, m] for q in range(SPLIT)] for c in range(2)]
            s02 = [z[c][0] + z[c][2] for c in range(2)]
            d02 = [z[c][0] - z[c][2] for c in range(2)]
            s13 = [z[c][1] + z[c][3] for c in range(2)]
            d13 = [z[c][1] - z[c][3] for c in range(2)]
            y = [
                (s02[0] + s13[0], s02[1] + s13[1]),
                (d02[0] + d13[1], d02[1] - d13[0]),
                (s02[0] - s13[0], s02[1] - s13[1]),
                (d02[0] - d13[1], d02[1] + d13[0]),
            ]
            for r in range(SPLIT):
                for c in range(2):
                    y_ref[
                        r,
                        m * ROWS : (m + 1) * ROWS,
                        pl.ds(pl.multiple_of(c * quarter + base, LANES), LANES),
                    ] = y[r][c].astype(jnp.bfloat16)
        return carry

    lax.fori_loop(0, quarter // LANES, chunk, 0)
    width = w_ref.shape[2]

    def transform(r, carry):
        z = jnp.dot(y_ref[r], w_ref[r], preferred_element_type=jnp.float32)
        own_ref[r] = z[: frames * ROWS].reshape(frames, ROWS, width)
        halo_ref[r] = z[frames * ROWS :].reshape(taps - 1, ROWS, width).astype(jnp.bfloat16)
        return carry

    lax.fori_loop(0, SPLIT, transform, 0)


def fir_dft(voltages, filter_taps, bins):
    local_inputs = voltages.shape[1]
    taps, fft = filter_taps.shape
    frames = voltages.shape[2] // fft
    outs = frames + taps - 1
    width = 2 * bins // SPLIT
    spread = jnp.broadcast_to(filter_taps[:, None, :], (taps, 8, fft))
    table = jnp.asarray(dft_table(fft, bins))
    once = pl.Buffered(1)

    def body(*refs):
        fir_dft_kernel(taps, frames, fft, *refs)

    return pl.pallas_call(
        body,
        grid=(local_inputs // ROWS,),
        in_specs=[
            pl.BlockSpec((2, ROWS, frames * fft), lambda i: (0, i, 0)),
            pl.BlockSpec((taps, 8, fft), lambda i: (0, 0, 0), pipeline_mode=once),
            pl.BlockSpec(table.shape, lambda i: (0, 0, 0), pipeline_mode=once),
        ],
        out_specs=[
            pl.BlockSpec((SPLIT, frames, ROWS, width), lambda i: (0, 0, i, 0)),
            pl.BlockSpec((SPLIT, taps - 1, ROWS, width), lambda i: (0, 0, i, 0)),
        ],
        out_shape=[
            jax.ShapeDtypeStruct((SPLIT, frames, local_inputs, width), jnp.float32),
            jax.ShapeDtypeStruct((SPLIT, taps - 1, local_inputs, width), jnp.bfloat16),
        ],
        scratch_shapes=[
            pltpu.VMEM((2, SPLIT, outs, ROWS, LANES), jnp.float32),
            pltpu.VMEM((SPLIT, outs * ROWS, 2 * fft // SPLIT), jnp.bfloat16),
        ],
        compiler_params=pltpu.CompilerParams(vmem_limit_bytes=56 * 2**20),
        cost_estimate=pl.CostEstimate(
            flops=2 * outs * local_inputs * 2 * fft * width,
            bytes_accessed=voltages.size * 2,
            transcendentals=0,
        ),
    )(voltages, spread, table)


def spectra(voltages, filter_taps, channels):
    local_inputs = voltages.shape[1]
    taps = filter_taps.shape[0]
    devices = lax.axis_size("stn")
    bins = devices * channels * AVG
    own, halo = fir_dft(voltages, filter_taps, bins)
    frames = own.shape[1]
    times = lax.axis_size("tm")
    arrived = lax.ppermute(halo, "tm", [(i, i + 1) for i in range(times - 1)])
    head = own[:, : taps - 1] + arrived.astype(jnp.float32)
    spectrum = jnp.concatenate([head, own[:, taps - 1 :]], axis=1).astype(jnp.bfloat16)
    per = AVG // SPLIT
    split = spectrum.reshape(SPLIT, frames, local_inputs, 2, devices, channels, per)
    return split.transpose(3, 2, 4, 5, 1, 0, 6).reshape(
        2, local_inputs, devices, channels * frames * AVG
    )


def shards(voltages, filter_taps, membership, block_active):
    channels = membership.shape[0]
    spectrum = spectra(voltages, filter_taps, channels)
    gathered = lax.all_to_all(spectrum, "stn", split_axis=2, concat_axis=1, tiled=True)
    inputs_all = gathered.shape[1]
    gathered = gathered.reshape(2, inputs_all, -1)
    depth = gathered.shape[2] // channels
    block = inputs_all // BLOCKS
    times = lax.axis_size("tm")
    own = lax.axis_index("tm")
    other = [gathered]
    for step in range(1, times):
        other.append(
            lax.ppermute(gathered, "tm", [(i, (i + step) % times) for i in range(times)])
        )
    rows = block // times
    scale = 1.0 / (depth * times)
    results = []
    for channel in range(channels):
        ids = jnp.repeat(membership[channel], 2)
        mine = lax.dynamic_slice_in_dim(ids.reshape(BLOCKS, block), own * rows, rows, 1)
        flags = block_active[channel].astype(jnp.float32)
        total = [0.0] * (BLOCKS * (BLOCKS + 1) // 2)
        for side in other:
            real, imag = side[:, :, channel * depth : (channel + 1) * depth]
            left = jnp.concatenate([real, imag], axis=1)
            swapped = jnp.concatenate([imag, -real], axis=1)
            both = jnp.stack([left, swapped]).reshape(2, BLOCKS, block, 2 * depth)
            both = lax.dynamic_slice_in_dim(both, own * rows, rows, 2)
            for upper in range(BLOCKS):
                product = lax.dot_general(
                    both[:, upper].reshape(2 * rows, 2 * depth),
                    left[: (upper + 1) * block],
                    (((1,), (1,)), ((), ())),
                    preferred_element_type=jnp.float32,
                ).reshape(2, rows, (upper + 1) * block)
                same = (mine[upper][:, None] == ids[None, : (upper + 1) * block]).astype(
                    jnp.float32
                )
                value = product * (scale * same)
                for lower in range(upper + 1):
                    pair = upper * (upper + 1) // 2 + lower
                    piece = value[:, :, lower * block : (lower + 1) * block] * flags[pair]
                    total[pair] = total[pair] + lax.reduce_precision(piece, 8, 7)
        results.append(jnp.stack(total))
    return jnp.stack(results)


def solution(mesh):
    placed = (P(None, "stn", "tm"), P(), P("stn", None), P("stn", None))
    return jax.shard_map(
        shards,
        mesh=mesh,
        in_specs=placed,
        out_specs=P("stn", None, None, "tm", None),
        check_vma=False,
    )
```

```python
import math

import jax
import jax.numpy as jnp
import numpy as np
from jax import lax
from jax.experimental import pallas as pl
from jax.experimental.pallas import tpu as pltpu
from jax.sharding import PartitionSpec as P

RADIX = 64
AVG = 16
BLOCKS = 4
ROWS = 16
LANES = 128
SPLIT = 4
PARTS = 2


def dft_table(fft, bins):
    quarter = fft // SPLIT
    count = bins // SPLIT
    n = np.arange(quarter)[:, None]
    parts = []
    for r in range(SPLIT):
        k = SPLIT * np.arange(count)[None, :] + r - bins // 2
        angle = 2.0 * math.pi * ((n * k) % fft) / fft
        c, s = np.cos(angle) / RADIX, np.sin(angle) / RADIX
        parts.append(np.block([[c, -s], [s, c]]))
    return np.stack(parts).astype(np.float32).astype(jnp.bfloat16)


def fir_dft_kernel(taps, frames, fft, v_ref, h_ref, w_ref, own_ref, halo_ref, filt, y_ref):
    quarter = fft // SPLIT
    outs = frames + taps - 1

    def chunk(g, carry):
        base = pl.multiple_of(g * LANES, LANES)
        for c in range(2):
            for q in range(SPLIT):
                at = [
                    pl.multiple_of(j * fft + q * quarter + base, LANES) for j in range(frames)
                ]
                v = [
                    v_ref[c, :, pl.ds(a, LANES)].astype(jnp.float32).reshape(2, 8, LANES)
                    for a in at
                ]
                col = pl.multiple_of(q * quarter + base, LANES)
                h = [h_ref[t, :, pl.ds(col, LANES)][None] for t in range(taps)]
                for m in range(outs):
                    acc = None
                    for j in range(max(0, m - taps + 1), min(frames - 1, m) + 1):
                        term = h[j - m + taps - 1] * v[j]
                        acc = term if acc is None else acc + term
                    filt[c, q, m] = acc.reshape(ROWS, LANES)
        for m in range(outs):
            z = [[filt[c, q, m] for q in range(SPLIT)] for c in range(2)]
            s02 = [z[c][0] + z[c][2] for c in range(2)]
            d02 = [z[c][0] - z[c][2] for c in range(2)]
            s13 = [z[c][1] + z[c][3] for c in range(2)]
            d13 = [z[c][1] - z[c][3] for c in range(2)]
            y = [
                (s02[0] + s13[0], s02[1] + s13[1]),
                (d02[0] + d13[1], d02[1] - d13[0]),
                (s02[0] - s13[0], s02[1] - s13[1]),
                (d02[0] - d13[1], d02[1] + d13[0]),
            ]
            for r in range(SPLIT):
                for c in range(2):
                    y_ref[
                        r,
                        m * ROWS : (m + 1) * ROWS,
                        pl.ds(pl.multiple_of(c * quarter + base, LANES), LANES),
                    ] = y[r][c].astype(jnp.bfloat16)
        return carry

    lax.fori_loop(0, quarter // LANES, chunk, 0)
    width = w_ref.shape[2]

    def transform(r, carry):
        z = jnp.dot(y_ref[r], w_ref[r], preferred_element_type=jnp.float32)
        own_ref[r] = z[: frames * ROWS].reshape(frames, ROWS, width)
        halo_ref[r] = z[frames * ROWS :].reshape(taps - 1, ROWS, width).astype(jnp.bfloat16)
        return carry

    lax.fori_loop(0, SPLIT, transform, 0)


def fir_dft(voltages, spread, table, part, parts):
    local_inputs = voltages.shape[1] // parts
    taps, _, fft = spread.shape
    frames = voltages.shape[2] // fft
    outs = frames + taps - 1
    width = table.shape[2]
    steps = local_inputs // ROWS
    once = pl.Buffered(1)

    def body(*refs):
        fir_dft_kernel(taps, frames, fft, *refs)

    return pl.pallas_call(
        body,
        grid=(steps,),
        in_specs=[
            pl.BlockSpec((2, ROWS, frames * fft), lambda i: (0, part * steps + i, 0)),
            pl.BlockSpec((taps, 8, fft), lambda i: (0, 0, 0), pipeline_mode=once),
            pl.BlockSpec(table.shape, lambda i: (0, 0, 0), pipeline_mode=once),
        ],
        out_specs=[
            pl.BlockSpec((SPLIT, frames, ROWS, width), lambda i: (0, 0, i, 0)),
            pl.BlockSpec((SPLIT, taps - 1, ROWS, width), lambda i: (0, 0, i, 0)),
        ],
        out_shape=[
            jax.ShapeDtypeStruct((SPLIT, frames, local_inputs, width), jnp.float32),
            jax.ShapeDtypeStruct((SPLIT, taps - 1, local_inputs, width), jnp.bfloat16),
        ],
        scratch_shapes=[
            pltpu.VMEM((2, SPLIT, outs, ROWS, LANES), jnp.float32),
            pltpu.VMEM((SPLIT, outs * ROWS, 2 * fft // SPLIT), jnp.bfloat16),
        ],
        compiler_params=pltpu.CompilerParams(vmem_limit_bytes=56 * 2**20),
        cost_estimate=pl.CostEstimate(
            flops=20 * outs * local_inputs * 2 * fft * width,
            bytes_accessed=voltages.size * 2 // parts,
            transcendentals=0,
        ),
    )(voltages, spread, table)


def with_history(own, halo):
    late = halo.shape[1]
    times = lax.axis_size("tm")
    arrived = lax.ppermute(halo, "tm", [(i, i + 1) for i in range(times - 1)])
    head = own[:, :late] + arrived.astype(jnp.float32)
    return jnp.concatenate([head, own[:, late:]], axis=1).astype(jnp.bfloat16)


def shards(voltages, filter_taps, membership, block_active):
    channels = membership.shape[0]
    devices, times = lax.axis_size("stn"), lax.axis_size("tm")
    local_inputs = voltages.shape[1]
    taps, fft = filter_taps.shape
    spread = jnp.broadcast_to(filter_taps[:, None, :], (taps, 8, fft))
    table = jnp.asarray(dft_table(fft, devices * channels * AVG))
    parts = min(PARTS, local_inputs // ROWS)
    made = [fir_dft(voltages, spread, table, part, parts) for part in range(parts)]
    spectrum = jnp.concatenate([with_history(*pair) for pair in made], axis=2)
    frames = spectrum.shape[1]
    depth = frames * AVG
    split = spectrum.reshape(
        SPLIT, frames, local_inputs, 2, devices, channels, AVG // SPLIT
    ).transpose(3, 2, 4, 5, 1, 0, 6)
    split = split.reshape(2, local_inputs, devices, channels * depth)
    landed = lax.all_to_all(split, "stn", split_axis=2, concat_axis=1, tiled=True)
    inputs_all = local_inputs * devices
    block = inputs_all // BLOCKS
    own = lax.axis_index("tm")
    rows = block // times
    scale = 1.0 / (depth * times)
    results = []
    for channel in range(channels):
        gathered = landed[..., channel * depth : (channel + 1) * depth].reshape(
            2, inputs_all, depth
        )
        other = [gathered]
        for step in range(1, times):
            around = [(i, (i + step) % times) for i in range(times)]
            other.append(lax.ppermute(gathered, "tm", around))
        ids = jnp.repeat(membership[channel], 2)
        mine = lax.dynamic_slice_in_dim(ids.reshape(BLOCKS, block), own * rows, rows, 1)
        flags = block_active[channel].astype(jnp.float32)
        total = [0.0] * (BLOCKS * (BLOCKS + 1) // 2)
        for side in other:
            real, imag = side
            left = jnp.concatenate([real, imag], axis=1)
            swapped = jnp.concatenate([imag, -real], axis=1)
            both = jnp.stack([left, swapped]).reshape(2, BLOCKS, block, 2 * depth)
            both = lax.dynamic_slice_in_dim(both, own * rows, rows, 2)
            for upper in range(BLOCKS):
                product = lax.dot_general(
                    both[:, upper].reshape(2 * rows, 2 * depth),
                    left[: (upper + 1) * block],
                    (((1,), (1,)), ((), ())),
                    preferred_element_type=jnp.float32,
                ).reshape(2, rows, (upper + 1) * block)
                same = (mine[upper][:, None] == ids[None, : (upper + 1) * block]).astype(
                    jnp.float32
                )
                value = product * (scale * same)
                for lower in range(upper + 1):
                    pair = upper * (upper + 1) // 2 + lower
                    piece = value[:, :, lower * block : (lower + 1) * block] * flags[pair]
                    total[pair] = total[pair] + lax.reduce_precision(piece, 8, 7)
        results.append(jnp.stack(total))
    return jnp.stack(results)


def solution(mesh):
    placed = (P(None, "stn", "tm"), P(), P("stn", None), P("stn", None))
    return jax.shard_map(
        shards,
        mesh=mesh,
        in_specs=placed,
        out_specs=P("stn", None, None, "tm", None),
        check_vma=False,
    )
```
